32 devices in a mesh: rhs: 4 (over y, x), rows: 8 (over z, core).
Axes of the slice: x: 2, y: 2, z: 4, core: 2. Of those that a mesh axis runs over, the one named last changes fastest.
Arguments:
- right_side: float32 [16384, 512], P('rows', 'rhs'), may hold values from -6 to 6
- fine_blocks: bfloat16 [128, 32, 128, 128], P('rows'), may hold values from -0.09375 to 0.09375
- fine_columns: int32 [128, 32], P('rows'), may hold values from 0 to 127, as said below
- fine_diag: float32 [16384], P('rows'), may hold values from 3 to 6
- aggregate: int32 [128], P('rows'), may hold values from 0 to 31, as said below
- coarse_blocks: float32 [32, 3, 128, 128], P(('rhs', 'rows')), may hold values from -0.3125 to 0.3125
- coarse_diag: float32 [4096], P(('rhs', 'rows')), may hold values from 1 to 2
Outputs:
- solution: float32 [16384, 512], P('rows', 'rhs')
The draws below stay inside these ranges and needn't reach their ends.
Inputs may be any that keep to these rules, and one draw needn't show every extreme that they name: `fine_columns`: the 32 stored blocks of fine block-row r have 32 distinct columns, each equal to r + o modulo 128 for an offset o from -16 to 16, and every row holds both end offsets. `aggregate`: fine block-row r maps to a coarse block c with c % (8) equal to r // 16; every coarse block receives one or more fine block-rows.
All inputs are finite; a program needn't handle non-finite values.
Results may differ from the reference program's by a relative error of at most 0.004.
Values may be sent and summed in bfloat16 or wider, within the bound.
A program may use at most 128 MiB of HBM per device.

```python
import jax
import jax.numpy as jnp
from jax import lax

B = 128
K = 32
BR_DEV = 16
CYCLES = 2
SWEEPS = 2
CHEB = 3
NB = 128
NF = 16384
NCB = 32
RHS = 512


def shuffle_band(row_key):
    return jax.random.permutation(row_key, K)


def draw_fine_columns(key, part):
    reach = K // 2
    block_ids = jnp.arange(NB, dtype=jnp.int32)[:, None]
    dropped = jax.random.randint(key, (NB, 1), 1 - reach, reach, dtype=jnp.int32)
    base = jnp.arange(K, dtype=jnp.int32)[None, :] - reach
    offsets = base + (base >= dropped).astype(jnp.int32)
    row_keys = jax.random.split(jax.random.fold_in(key, 3), NB)
    orders = jax.vmap(shuffle_band)(row_keys)
    offsets = jnp.take_along_axis(offsets, orders, axis=1)
    return jnp.mod(block_ids + offsets, NB).astype(jnp.int32)


def shuffle_row(row_key):
    return jax.random.permutation(row_key, BR_DEV)


def draw_aggregate(key, part):
    device_rows = NB // BR_DEV
    groups = NCB // device_rows
    group_ids = jax.random.randint(key, (device_rows, BR_DEV), 0, groups, dtype=jnp.int32)
    group_ids = group_ids.at[:, :groups].set(jnp.arange(groups, dtype=jnp.int32)[None, :])
    row_keys = jax.random.split(jax.random.fold_in(key, 7), device_rows)
    orders = jax.vmap(shuffle_row)(row_keys)
    group_ids = jnp.take_along_axis(group_ids, orders, axis=1)
    owners = jnp.arange(device_rows, dtype=jnp.int32)[:, None]
    return (group_ids * device_rows + owners).reshape(NB).astype(jnp.int32)


def level_of(rng, dims, shards, least, largest):
    def one(dim, shards_of):
        steps = jax.random.uniform(jax.random.fold_in(jax.random.fold_in(rng, 6), dim), (shards_of,), jnp.float32, least / len(shards), largest / len(shards))
        return jnp.repeat(jnp.exp(steps), dims[dim] // shards_of).reshape((-1,) + (1,) * (len(dims) - dim - 1))

    gain = one(*shards[0])
    for cut in shards[1:]:
        gain = gain * one(*cut)
    return gain


def bell_draw(key, extent, scale, bound, shards=(), kind=jnp.bfloat16):
    entries = jax.random.normal(key, extent, jnp.float32) * scale
    if len(shards) > 0:
        entries = level_of(key, extent, shards, -0.22, 0.18) * entries
    return jnp.clip(entries, min=-bound, max=bound).astype(kind)


def setup_inputs(seed: int = 0) -> dict:
    arg_keys = jax.random.split(jax.random.key(seed), 8)
    right_side = bell_draw(arg_keys[0], (NF, RHS), 1.0, 6.0, ((0, 8), (1, 4)), jnp.float32)
    fine_blocks = bell_draw(arg_keys[1], (NB, K, B, B), (K * B) ** -0.5, 0.09375, ((0, 8),))
    fine_columns = draw_fine_columns(jax.random.fold_in(arg_keys[7], 71), 0)
    fine_diag = jnp.clip(3.0 + 3.0 * jax.random.uniform(arg_keys[3], (NF,), jnp.float32) ** level_of(arg_keys[3], (NF,), ((0, 8),), -0.2, 0.2), 3.0, 6.0)
    aggregate = draw_aggregate(jax.random.fold_in(arg_keys[7], 71), 0)
    coarse_blocks = bell_draw(arg_keys[5], (NCB, 3, B, B), (3 * B) ** -0.5, 0.3125, ((0, 32),), jnp.float32)
    coarse_diag = jnp.clip(1.0 + 1.0 * jax.random.uniform(arg_keys[6], (NCB * B,), jnp.float32) ** level_of(arg_keys[6], (NCB * B,), ((0, 32),), -0.2, 0.2), 1.0, 2.0)
    return dict(right_side=right_side, fine_blocks=fine_blocks, fine_columns=fine_columns, fine_diag=fine_diag, aggregate=aggregate, coarse_blocks=coarse_blocks, coarse_diag=coarse_diag)


relax_weight = 0.7
centre = 1.0
half_width = 0.6


def fine_apply(field, fine_blocks, fine_columns, fine_scale):
    rounded = field.astype(jnp.bfloat16)

    def one_row(pair):
        row_blocks, row_columns = pair
        picked = rounded[row_columns].astype(jnp.float32)
        return jnp.einsum("kij,kjn->in", row_blocks.astype(jnp.float32), picked)

    product = lax.map(one_row, (fine_blocks, fine_columns))
    return fine_scale * field + product


def coarse_apply(field, coarse_blocks, coarse_scale):
    empty = jnp.zeros((1,) + field.shape[1:], jnp.float32)
    lower_rim = jnp.concatenate([empty, field[:-1]], axis=0)
    upper_rim = jnp.concatenate([field[1:], empty], axis=0)
    high = lax.Precision.HIGHEST
    total = coarse_scale * field
    total = total + jnp.einsum("cij,cjn->cin", coarse_blocks[:, 0], lower_rim, precision=high)
    total = total + jnp.einsum("cij,cjn->cin", coarse_blocks[:, 1], field, precision=high)
    total = total + jnp.einsum("cij,cjn->cin", coarse_blocks[:, 2], upper_rim, precision=high)
    return total


def chebyshev(source, coarse_blocks, coarse_scale):
    sigma_ratio = centre / half_width
    ratio_old = 1.0 / sigma_ratio
    update = source / coarse_scale / centre
    correction = update
    for step_index in range(CHEB - 1):
        ratio_new = 1.0 / (2.0 * sigma_ratio - ratio_old)
        scaled = (source - coarse_apply(correction, coarse_blocks, coarse_scale)) / coarse_scale
        update = ratio_new * ratio_old * update + (2.0 * ratio_new / half_width) * scaled
        correction = correction + update
        ratio_old = ratio_new
    return correction


def reference(right_side, fine_blocks, fine_columns, fine_diag, aggregate, coarse_blocks, coarse_diag):
    source = right_side.reshape(NB, B, RHS)
    fine_scale = fine_diag.reshape(NB, B, 1)
    coarse_scale = coarse_diag.reshape(NCB, B, 1)
    solution = jnp.zeros((NB, B, RHS), jnp.float32)
    for turn_index in range(CYCLES):
        for sweep_index in range(SWEEPS):
            if turn_index == 0 and sweep_index == 0:
                solution = relax_weight * source / fine_scale
            else:
                solution = solution + relax_weight * (source - fine_apply(solution, fine_blocks, fine_columns, fine_scale)) / fine_scale
        residual = source - fine_apply(solution, fine_blocks, fine_columns, fine_scale)
        coarse_side = jax.ops.segment_sum(residual, aggregate, num_segments=NCB)
        correction = chebyshev(coarse_side, coarse_blocks, coarse_scale)
        solution = solution + correction[aggregate]
        for sweep_index in range(SWEEPS):
            solution = solution + relax_weight * (source - fine_apply(solution, fine_blocks, fine_columns, fine_scale)) / fine_scale
    return solution.reshape(NF, RHS)
```

```python
import functools

import jax
import jax.numpy as jnp
from jax import lax
from jax.experimental import pallas as pl
from jax.experimental.pallas import tpu as pltpu
from jax.sharding import PartitionSpec as P

CYCLES = 2
SWEEPS = 2
CHEB = 3
relax_weight = 0.7
centre = 1.0
half_width = 0.6

PARTS = 4
STAGES = 4
MESH = pl.DeviceIdType.MESH
F32 = jnp.float32
BF16 = jnp.bfloat16


def kernel(
    geo,
    table,
    source_ref,
    blocks_ref,
    diag_ref,
    mask_ref,
    coarse_ref,
    cdiag_ref,
    out_ref,
    *scratch,
):
    n_rows, n_rhs, block_rows, stored, size = geo
    stages = scratch[:STAGES]
    (
        band,
        xown,
        xleft,
        xright,
        acc,
        rhs,
        weight,
        diag,
        lmask,
        rmask,
        cops,
        cdiags,
        cinv,
        csource,
        ccorr,
        cupd,
        csend,
        lrim,
        rrim,
        stage_sem,
        fsend_sem,
        frecv_sem,
        csend_sem,
        crecv_sem,
        msend_sem,
        mrecv_sem,
        gsend_sem,
        grecv_sem,
    ) = scratch[STAGES:]
    per = block_rows // PARTS
    part = per * size
    groups = n_rhs
    wide = stored + per
    me = lax.axis_index("rows")
    mine = lax.axis_index("rhs")
    right = lax.rem(me + 1, n_rows)
    left = lax.rem(me + n_rows - 1, n_rows)
    low_shift = (me + n_rows - 1) // n_rows
    high_shift = (me + 1) // n_rows

    def stage_copy(row, s):
        return pltpu.make_async_copy(
            blocks_ref.at[row], stages[s].at[pl.ds(0, stored)], stage_sem.at[s]
        )

    for s in range(STAGES):
        stage_copy(s, s).start()

    barrier = pltpu.get_barrier_semaphore()
    for other in (left, right):
        pl.semaphore_signal(barrier, inc=1, device_id={"rows": other}, device_id_type=MESH)
    for step in range(1, n_rhs):
        peer = lax.rem(mine + step, n_rhs)
        pl.semaphore_signal(barrier, inc=1, device_id={"rhs": peer}, device_id_type=MESH)

    for r in range(block_rows):
        rows = pl.ds(r * size, size)
        column = jnp.broadcast_to(diag_ref[pl.ds(r, 1), :], (size, size)).T
        diag[rows, :] = column
        scale = relax_weight / column
        weight[rows, :] = scale
        value = source_ref[rows, :]
        rhs[0, rows, :] = value
        value = scale * value
        out_ref[rows, :] = value
        xown[0, r // per, pl.ds((r % per) * size, size), :] = value.astype(BF16)
    cops[mine] = coarse_ref[...].astype(BF16)
    cdiags[mine] = cdiag_ref[...]
    zero = jnp.zeros((size, size), BF16)
    for s in range(STAGES):
        stages[s][stored] = zero
    for t in range(CHEB):
        lrim[t, 0] = zero
        rrim[t, groups] = zero
    pl.semaphore_wait(barrier, n_rhs + 1)

    def fine_copy(way, slot, c):
        return pltpu.make_async_remote_copy(
            src_ref=xown.at[slot, c],
            dst_ref=(xleft if way == 0 else xright).at[slot, c],
            send_sem=fsend_sem.at[way, slot, c],
            recv_sem=frecv_sem.at[way, slot, c],
            device_id={"rows": right if way == 0 else left},
            device_id_type=MESH,
        )

    def coarse_copy(way, t):
        return pltpu.make_async_remote_copy(
            src_ref=csend.at[t],
            dst_ref=lrim.at[t, pl.ds(1, groups)] if way == 0 else rrim.at[t, pl.ds(0, groups)],
            send_sem=csend_sem.at[way, t],
            recv_sem=crecv_sem.at[way, t],
            device_id={"rows": right if way == 0 else left},
            device_id_type=MESH,
        )

    def mask_copy(way):
        return pltpu.make_async_remote_copy(
            src_ref=mask_ref,
            dst_ref=lmask if way == 0 else rmask,
            send_sem=msend_sem.at[way],
            recv_sem=mrecv_sem.at[way],
            device_id={"rows": right if way == 0 else left},
            device_id_type=MESH,
        )

    def gather_copies(step):
        peer = lax.rem(mine + step, n_rhs)
        return [
            pltpu.make_async_remote_copy(
                src_ref=whole.at[mine],
                dst_ref=whole.at[mine],
                send_sem=gsend_sem.at[k, step - 1],
                recv_sem=grecv_sem.at[k, step - 1],
                device_id={"rhs": peer},
                device_id_type=MESH,
            )
            for k, whole in enumerate((cops, cdiags))
        ]

    middle = list(range(1, PARTS - 1))

    def send_part(slot, c):
        fine_copy(0, slot, c).start()
        fine_copy(1, slot, c).start()

    for c in middle:
        send_part(0, c)
    fine_copy(0, 0, PARTS - 1).start()
    fine_copy(1, 0, 0).start()
    fine_copy(0, 0, 0).start()
    fine_copy(1, 0, PARTS - 1).start()
    for way in (0, 1):
        mask_copy(way).start()
    for step in range(1, n_rhs):
        for copy in gather_copies(step):
            copy.start()

    rounds = block_rows // STAGES

    def lay(turn, carry):
        for s in range(STAGES):
            row = turn * STAGES + s
            stage_copy(row, s).wait()
            rows = pl.ds(pl.multiple_of(row * size, size), size)
            for j in range(wide):
                band[rows, pl.ds(j * size, size)] = stages[s][table[row * wide + j]]

            @pl.when(turn < rounds - 1)
            def _():
                stage_copy(row + STAGES, s).start()

        return carry

    lax.fori_loop(0, rounds, lay, 0)

    for way in (0, 1):
        mask_copy(way).wait()
    for step in range(1, n_rhs):
        for copy in gather_copies(step):
            copy.wait()
    for q in range(groups):
        row = cdiags[q][0:1, :]
        cinv[q] = 1.0 / jnp.broadcast_to(row, (size, size)).T

    def rows_of(g):
        return pl.ds(g * part, part)

    def times(g, first, count, x):
        lhs = band[rows_of(g), pl.ds(first * part, count * part)]
        return jnp.dot(lhs, x, preferred_element_type=F32)

    def spread(marks, l, fields):
        total = None
        for q in range(groups):
            term = marks[pl.ds(l * groups + q, 1), :] * fields[q].astype(F32)
            total = term if total is None else total + term
        return total

    def coarse_solve(slot):
        for q in range(groups):
            total = jnp.zeros((size, size), F32)
            for r in range(block_rows):
                total += mask_ref[pl.ds(r * groups + q, 1), :] * rhs[1, pl.ds(r * size, size), :]
            csource[q] = total
            first = total * cinv[q] / centre
            cupd[q] = first
            ccorr[q] = first
            csend[0, q] = first.astype(BF16)
        coarse_copy(0, 0).start()
        coarse_copy(1, 0).start()
        sigma = centre / half_width
        old = 1.0 / sigma
        for t in range(CHEB - 1):
            new = 1.0 / (2.0 * sigma - old)
            for q in range(groups):
                acc[pl.ds(q * size, size), :] = jnp.dot(
                    cops[q, 1], csend[t, q], preferred_element_type=F32
                )
            coarse_copy(0, t).wait_recv()
            coarse_copy(1, t).wait_recv()
            for q in range(groups):
                value = acc[pl.ds(q * size, size), :]
                value += jnp.dot(cops[q, 0], lrim[t, q + low_shift], preferred_element_type=F32)
                value += jnp.dot(cops[q, 2], rrim[t, q + high_shift], preferred_element_type=F32)
                corr = ccorr[q]
                scaled = (csource[q] - value) * cinv[q] - corr
                update = new * old * cupd[q] + (2.0 * new / half_width) * scaled
                corr = corr + update
                cupd[q] = update
                ccorr[q] = corr
                csend[t + 1, q] = corr.astype(BF16)
            coarse_copy(0, t + 1).start()
            coarse_copy(1, t + 1).start()
            old = new
        fields = [ccorr.at[q] for q in range(groups)]
        for r in range(block_rows):
            rows = pl.ds(r * size, size)
            value = spread(mask_ref, r, [f[...] for f in fields])
            out_ref[rows, :] = out_ref[rows, :] + (1.0 - relax_weight) * value
            xown[slot, r // per, pl.ds((r % per) * size, size), :] = value.astype(BF16)

    applies = CYCLES * (2 * SWEEPS + 1) - 1
    turn_len = 2 * SWEEPS + 1

    def apply(e, carry):
        slot = lax.rem(e, 2)
        after = 1 - slot
        place = lax.rem(e + 1, turn_len)
        is_residual = place == SWEEPS
        is_first_post = place == SWEEPS + 1
        keep = jnp.where(is_first_post, 1.0, 1.0 - relax_weight).astype(F32)
        side = jnp.where(is_first_post, 1, 0)

        own = xown[slot].reshape(PARTS * part, size)
        for g in range(PARTS):
            acc[rows_of(g), :] = times(g, PARTS - g, PARTS, own)

        @pl.when(is_first_post)
        def _():
            t = CHEB - 1
            for way in (0, 1):
                coarse_copy(way, t).wait_recv()
                rim, marks, halo = ((lrim, lmask, xleft), (rrim, rmask, xright))[way]
                first = 1 if way == 0 else 0
                for r in range(block_rows):
                    value = spread(marks, r, [rim[t, first + q] for q in range(groups)])
                    halo[slot, r // per, pl.ds((r % per) * size, size), :] = value.astype(BF16)
                for k in range(CHEB):
                    coarse_copy(way, k).wait_send()

        def await_part(way, c):
            @pl.when(jnp.logical_not(is_first_post))
            def _():
                fine_copy(way, slot, c).wait_recv()

        def add_left(c):
            await_part(0, c)
            x = xleft[slot, c]
            for g in range(c + 1):
                acc[rows_of(g), :] += times(g, c - g, 1, x)

        def add_right(c):
            await_part(1, c)
            x = xright[slot, c]
            for g in range(c, PARTS):
                acc[rows_of(g), :] += times(g, 2 * PARTS + c - g, 1, x)

        def finish(g):
            rows = rows_of(g)

            @pl.when(is_residual)
            def _():
                rhs[1, rows, :] = rhs[0, rows, :] - diag[rows, :] * out_ref[rows, :] - acc[rows, :]

            @pl.when(jnp.logical_not(is_residual))
            def _():
                value = keep * out_ref[rows, :] + weight[rows, :] * (rhs[side, rows, :] - acc[rows, :])
                out_ref[rows, :] = value
                xown[after, g] = value.astype(BF16)

        sends = jnp.logical_and(jnp.logical_not(is_residual), e < applies - 1)
        for c in middle:
            add_right(c)
            add_left(PARTS - 1 - c)
        add_left(PARTS - 1)
        add_right(0)
        for g in middle:
            finish(g)

        @pl.when(sends)
        def _():
            for g in middle:
                send_part(after, g)

        add_left(0)
        add_right(PARTS - 1)
        finish(PARTS - 1)
        finish(0)

        @pl.when(sends)
        def _():
            fine_copy(0, after, PARTS - 1).start()
            fine_copy(1, after, 0).start()
            fine_copy(0, after, 0).start()
            fine_copy(1, after, PARTS - 1).start()

        @pl.when(jnp.logical_not(is_first_post))
        def _():
            for way in (0, 1):
                for c in range(PARTS):
                    fine_copy(way, slot, c).wait_send()

        @pl.when(is_residual)
        def _():
            coarse_solve(after)

        return carry

    lax.fori_loop(0, applies, apply, 0)


def shards(right_side, fine_blocks, fine_columns, fine_diag, aggregate, coarse_blocks, coarse_diag):
    block_rows, stored, size, _ = fine_blocks.shape
    n_rows = lax.axis_size("rows")
    n_rhs = lax.axis_size("rhs")
    total_blocks = block_rows * n_rows
    groups = n_rhs * coarse_blocks.shape[0]
    per = block_rows // PARTS
    part = per * size
    wide = stored + per
    reach = stored // 2

    local = jnp.arange(block_rows, dtype=jnp.int32)[:, None]
    first = lax.axis_index("rows") * block_rows
    places = jnp.mod(fine_columns - (first + local) + reach, total_blocks) + local % per
    hit = places[:, None, :] == jnp.arange(wide, dtype=jnp.int32)[None, :, None]
    order = jnp.arange(stored, dtype=jnp.int32)[None, None, :]
    found = jnp.max(jnp.where(hit, order, -1), axis=2)
    table = jnp.where(found < 0, stored, found).reshape(block_rows * wide)

    group_id = aggregate // n_rows
    marks = (group_id[:, None] == jnp.arange(groups, dtype=jnp.int32)[None, :]).astype(F32)
    marks = jnp.broadcast_to(marks[:, :, None], (block_rows, groups, size))
    marks = marks.reshape(block_rows * groups, size)
    coarse_rows = jnp.broadcast_to(coarse_diag[None, :], (8, size))

    vmem = pl.BlockSpec(memory_space=pltpu.VMEM)
    field = PARTS * part
    geo = (n_rows, n_rhs, block_rows, stored, size)
    return pl.pallas_call(
        functools.partial(kernel, geo),
        out_shape=jax.ShapeDtypeStruct((field, size), F32),
        in_specs=[
            pl.BlockSpec(memory_space=pltpu.SMEM),
            vmem,
            pl.BlockSpec(memory_space=pl.ANY),
            vmem,
            vmem,
            vmem,
            vmem,
        ],
        out_specs=vmem,
        scratch_shapes=[pltpu.VMEM((stored + 1, size, size), BF16) for _ in range(STAGES)]
        + [
            pltpu.VMEM((field, wide * size), BF16),
            pltpu.VMEM((2, PARTS, part, size), BF16),
            pltpu.VMEM((2, PARTS, part, size), BF16),
            pltpu.VMEM((2, PARTS, part, size), BF16),
            pltpu.VMEM((field, size), F32),
            pltpu.VMEM((2, field, size), F32),
            pltpu.VMEM((field, size), F32),
            pltpu.VMEM((field, size), F32),
            pltpu.VMEM((block_rows * groups, size), F32),
            pltpu.VMEM((block_rows * groups, size), F32),
            pltpu.VMEM((groups, 3, size, size), BF16),
            pltpu.VMEM((groups, 8, size), F32),
            pltpu.VMEM((groups, size, size), F32),
            pltpu.VMEM((groups, size, size), F32),
            pltpu.VMEM((groups, size, size), F32),
            pltpu.VMEM((groups, size, size), F32),
            pltpu.VMEM((CHEB, groups, size, size), BF16),
            pltpu.VMEM((CHEB, groups + 1, size, size), BF16),
            pltpu.VMEM((CHEB, groups + 1, size, size), BF16),
            pltpu.SemaphoreType.DMA((STAGES,)),
            pltpu.SemaphoreType.DMA((2, 2, PARTS)),
            pltpu.SemaphoreType.DMA((2, 2, PARTS)),
            pltpu.SemaphoreType.DMA((2, CHEB)),
            pltpu.SemaphoreType.DMA((2, CHEB)),
            pltpu.SemaphoreType.DMA((2,)),
            pltpu.SemaphoreType.DMA((2,)),
            pltpu.SemaphoreType.DMA((2, n_rhs - 1)),
            pltpu.SemaphoreType.DMA((2, n_rhs - 1)),
        ],
        compiler_params=pltpu.CompilerParams(
            collective_id=0, has_side_effects=True, vmem_limit_bytes=56 * 1024 * 1024
        ),
    )(
        table,
        right_side,
        fine_blocks,
        fine_diag.reshape(block_rows, size),
        marks,
        coarse_blocks[0],
        coarse_rows,
    )


def solution(mesh):
    in_specs = (
        P("rows", "rhs"),
        P("rows", None, None, None),
        P("rows", None),
        P("rows"),
        P("rows"),
        P(("rhs", "rows"), None, None, None),
        P(("rhs", "rows")),
    )
    out_specs = P("rows", "rhs")
    return jax.shard_map(shards, mesh=mesh, in_specs=in_specs, out_specs=out_specs, check_vma=False)
```

```python
import functools

import jax
import jax.numpy as jnp
from jax import lax
from jax.experimental import pallas as pl
from jax.experimental.pallas import tpu as pltpu
from jax.sharding import PartitionSpec as P

CYCLES = 2
SWEEPS = 2
CHEB = 3
relax_weight = 0.7
centre = 1.0
half_width = 0.6

PARTS = 4
STAGES = 4
MESH = pl.DeviceIdType.MESH
F32 = jnp.float32
BF16 = jnp.bfloat16


def kernel(
    geo,
    table,
    source_ref,
    blocks_ref,
    diag_ref,
    aggregate_ref,
    coarse_ref,
    cdiag_ref,
    out_ref,
    *scratch,
):
    n_rows, n_rhs, block_rows, stored, size = geo
    stages = scratch[:STAGES]
    (
        band,
        xown,
        xleft,
        xright,
        acc,
        rhs,
        weight,
        diag,
        lmask,
        rmask,
        mask_ref,
        cops,
        cdiags,
        cinv,
        csource,
        ccorr,
        cupd,
        csend,
        lrim,
        rrim,
        stage_sem,
        fsend_sem,
        frecv_sem,
        csend_sem,
        crecv_sem,
        msend_sem,
        mrecv_sem,
        gsend_sem,
        grecv_sem,
    ) = scratch[STAGES:]
    per = block_rows // PARTS
    part = per * size
    groups = n_rhs
    wide = stored + per
    me = lax.axis_index("rows")
    mine = lax.axis_index("rhs")
    right = lax.rem(me + 1, n_rows)
    left = lax.rem(me + n_rows - 1, n_rows)
    low_shift = (me + n_rows - 1) // n_rows
    high_shift = (me + 1) // n_rows

    def stage_copy(row, s):
        return pltpu.make_async_copy(
            blocks_ref.at[row], stages[s].at[pl.ds(0, stored)], stage_sem.at[s]
        )

    for s in range(STAGES):
        stage_copy(s, s).start()

    barrier = pltpu.get_barrier_semaphore()
    for other in (left, right):
        pl.semaphore_signal(barrier, inc=1, device_id={"rows": other}, device_id_type=MESH)
    for step in range(1, n_rhs):
        peer = lax.rem(mine + step, n_rhs)
        pl.semaphore_signal(barrier, inc=1, device_id={"rhs": peer}, device_id_type=MESH)

    def fine_copy(way, slot, c):
        return pltpu.make_async_remote_copy(
            src_ref=xown.at[slot, c],
            dst_ref=(xleft if way == 0 else xright).at[slot, c],
            send_sem=fsend_sem.at[way, slot, c],
            recv_sem=frecv_sem.at[way, slot, c],
            device_id={"rows": right if way == 0 else left},
            device_id_type=MESH,
        )

    def coarse_copy(way, t, q):
        return pltpu.make_async_remote_copy(
            src_ref=csend.at[t, q],
            dst_ref=lrim.at[t, 1 + q] if way == 0 else rrim.at[t, q],
            send_sem=csend_sem.at[way, t, q],
            recv_sem=crecv_sem.at[way, t, q],
            device_id={"rows": right if way == 0 else left},
            device_id_type=MESH,
        )

    def mask_copy(way):
        return pltpu.make_async_remote_copy(
            src_ref=mask_ref,
            dst_ref=lmask if way == 0 else rmask,
            send_sem=msend_sem.at[way],
            recv_sem=mrecv_sem.at[way],
            device_id={"rows": right if way == 0 else left},
            device_id_type=MESH,
        )

    def gather_copies(step):
        peer = lax.rem(mine + step, n_rhs)
        return [
            pltpu.make_async_remote_copy(
                src_ref=whole.at[mine],
                dst_ref=whole.at[mine],
                send_sem=gsend_sem.at[k, step - 1],
                recv_sem=grecv_sem.at[k, step - 1],
                device_id={"rhs": peer},
                device_id_type=MESH,
            )
            for k, whole in enumerate((cops, cdiags))
        ]

    middle = list(range(1, PARTS - 1))

    def send_part(slot, c):
        fine_copy(0, slot, c).start()
        fine_copy(1, slot, c).start()

    def begin(c):
        for r in range(c * per, (c + 1) * per):
            rows = pl.ds(r * size, size)
            column = jnp.broadcast_to(diag_ref[pl.ds(r, 1), :], (size, size)).T
            diag[rows, :] = column
            scale = relax_weight / column
            weight[rows, :] = scale
            value = source_ref[rows, :]
            rhs[0, rows, :] = value
            value = scale * value
            out_ref[rows, :] = value
            xown[0, c, pl.ds((r % per) * size, size), :] = value.astype(BF16)

    for c in middle:
        begin(c)
    pl.semaphore_wait(barrier, n_rhs + 1)
    for c in middle:
        send_part(0, c)
    begin(PARTS - 1)
    begin(0)
    fine_copy(0, 0, PARTS - 1).start()
    fine_copy(1, 0, 0).start()
    fine_copy(0, 0, 0).start()
    fine_copy(1, 0, PARTS - 1).start()

    cops[mine] = coarse_ref[...].astype(BF16)
    cdiags[mine] = jnp.broadcast_to(cdiag_ref[...], (8, size))
    for step in range(1, n_rhs):
        for copy in gather_copies(step):
            copy.start()
    zero = jnp.zeros((size, size), BF16)
    for s in range(STAGES):
        stages[s][stored] = zero
    for t in range(CHEB):
        lrim[t, 0] = zero
        rrim[t, groups] = zero
    for r in range(block_rows):
        for q in range(groups):
            mark = jnp.where(aggregate_ref[r] == q * n_rows + me, 1.0, 0.0).astype(F32)
            mask_ref[pl.ds(r * groups + q, 1), :] = jnp.full((1, size), mark, F32)
    for way in (0, 1):
        mask_copy(way).start()

    rounds = block_rows // STAGES

    def lay(turn, carry):
        for s in range(STAGES):
            row = turn * STAGES + s
            stage_copy(row, s).wait()
            rows = pl.ds(pl.multiple_of(row * size, size), size)
            for j in range(wide):
                band[rows, pl.ds(j * size, size)] = stages[s][table[row * wide + j]]

            @pl.when(turn < rounds - 1)
            def _():
                stage_copy(row + STAGES, s).start()

        return carry

    lax.fori_loop(0, rounds, lay, 0)

    for way in (0, 1):
        mask_copy(way).wait()
    for step in range(1, n_rhs):
        for copy in gather_copies(step):
            copy.wait()
    for q in range(groups):
        row = cdiags[q][0:1, :]
        cinv[q] = 1.0 / jnp.broadcast_to(row, (size, size)).T

    def rows_of(g):
        return pl.ds(g * part, part)

    def times(g, first, count, x):
        lhs = band[rows_of(g), pl.ds(first * part, count * part)]
        return jnp.dot(lhs, x, preferred_element_type=F32)

    def spread(marks, l, fields):
        total = None
        for q in range(groups):
            term = marks[pl.ds(l * groups + q, 1), :] * fields[q].astype(F32)
            total = term if total is None else total + term
        return total

    def coarse_solve(slot):
        for q in range(groups):
            total = jnp.zeros((size, size), F32)
            for r in range(block_rows):
                total += mask_ref[pl.ds(r * groups + q, 1), :] * rhs[1, pl.ds(r * size, size), :]
            csource[q] = total
            first = total * cinv[q] / centre
            cupd[q] = first
            ccorr[q] = first
            csend[0, q] = first.astype(BF16)
            coarse_copy(0, 0, q).start()
            coarse_copy(1, 0, q).start()
        sigma = centre / half_width
        old = 1.0 / sigma
        for t in range(CHEB - 1):
            new = 1.0 / (2.0 * sigma - old)
            for q in range(groups):
                acc[pl.ds(q * size, size), :] = jnp.dot(
                    cops[q, 1], csend[t, q], preferred_element_type=F32
                )
            coarse_copy(1, t, 0).wait_recv()
            for q in range(groups):
                coarse_copy(0, t, q).wait_recv()
                if q + 1 < groups:
                    coarse_copy(1, t, q + 1).wait_recv()
                value = acc[pl.ds(q * size, size), :]
                value += jnp.dot(cops[q, 0], lrim[t, q + low_shift], preferred_element_type=F32)
                value += jnp.dot(cops[q, 2], rrim[t, q + high_shift], preferred_element_type=F32)
                corr = ccorr[q]
                scaled = (csource[q] - value) * cinv[q] - corr
                update = new * old * cupd[q] + (2.0 * new / half_width) * scaled
                corr = corr + update
                cupd[q] = update
                ccorr[q] = corr
                csend[t + 1, q] = corr.astype(BF16)
                coarse_copy(0, t + 1, q).start()
                coarse_copy(1, t + 1, q).start()
            old = new
        fields = [ccorr.at[q] for q in range(groups)]
        for r in range(block_rows):
            rows = pl.ds(r * size, size)
            value = spread(mask_ref, r, [f[...] for f in fields])
            out_ref[rows, :] = out_ref[rows, :] + (1.0 - relax_weight) * value
            xown[slot, r // per, pl.ds((r % per) * size, size), :] = value.astype(BF16)

    applies = CYCLES * (2 * SWEEPS + 1) - 1
    turn_len = 2 * SWEEPS + 1

    def apply(e, carry):
        slot = lax.rem(e, 2)
        after = 1 - slot
        place = lax.rem(e + 1, turn_len)
        is_residual = place == SWEEPS
        is_first_post = place == SWEEPS + 1
        keep = jnp.where(is_first_post, 1.0, 1.0 - relax_weight).astype(F32)
        side = jnp.where(is_first_post, 1, 0)

        own = xown[slot].reshape(PARTS * part, size)
        for g in range(PARTS):
            acc[rows_of(g), :] = times(g, PARTS - g, PARTS, own)

        def relax(g):
            rows = rows_of(g)
            value = keep * out_ref[rows, :] + weight[rows, :] * (rhs[side, rows, :] - acc[rows, :])
            out_ref[rows, :] = value
            xown[after, g] = value.astype(BF16)

        @pl.when(is_first_post)
        def _():
            t = CHEB - 1
            for way in (0, 1):
                rim, marks, halo = ((lrim, lmask, xleft), (rrim, rmask, xright))[way]
                first = 1 if way == 0 else 0
                for q in range(groups):
                    coarse_copy(way, t, q).wait_recv()
                for r in range(block_rows):
                    value = spread(marks, r, [rim[t, first + q] for q in range(groups)])
                    halo[slot, r // per, pl.ds((r % per) * size, size), :] = value.astype(BF16)
            for g in middle + [PARTS - 1, 0]:
                lower = xleft[slot, pl.ds(g, PARTS - g)].reshape((PARTS - g) * part, size)
                upper = xright[slot, pl.ds(0, g + 1)].reshape((g + 1) * part, size)
                acc[rows_of(g), :] += times(g, 0, PARTS - g, lower) + times(
                    g, 2 * PARTS - g, g + 1, upper
                )
                relax(g)
                send_part(after, g)
            for way in (0, 1):
                for k in range(CHEB):
                    for q in range(groups):
                        coarse_copy(way, k, q).wait_send()

        @pl.when(jnp.logical_not(is_first_post))
        def _():
            def add_left(c):
                fine_copy(0, slot, c).wait_recv()
                x = xleft[slot, c]
                for g in range(c + 1):
                    acc[rows_of(g), :] += times(g, c - g, 1, x)

            def add_right(c):
                fine_copy(1, slot, c).wait_recv()
                x = xright[slot, c]
                for g in range(c, PARTS):
                    acc[rows_of(g), :] += times(g, 2 * PARTS + c - g, 1, x)

            def finish(g):
                rows = rows_of(g)

                @pl.when(is_residual)
                def _():
                    rhs[1, rows, :] = rhs[0, rows, :] - diag[rows, :] * out_ref[rows, :] - acc[rows, :]

                @pl.when(jnp.logical_not(is_residual))
                def _():
                    relax(g)

            sends = jnp.logical_and(jnp.logical_not(is_residual), e < applies - 1)
            for c in middle:
                add_right(c)
                add_left(PARTS - 1 - c)
            add_left(PARTS - 1)
            add_right(0)
            for g in middle:
                finish(g)

            @pl.when(sends)
            def _():
                for g in middle:
                    send_part(after, g)

            add_left(0)
            add_right(PARTS - 1)
            finish(PARTS - 1)
            finish(0)

            @pl.when(sends)
            def _():
                fine_copy(0, after, PARTS - 1).start()
                fine_copy(1, after, 0).start()
                fine_copy(0, after, 0).start()
                fine_copy(1, after, PARTS - 1).start()

            for way in (0, 1):
                for c in range(PARTS):
                    fine_copy(way, slot, c).wait_send()

        @pl.when(is_residual)
        def _():
            coarse_solve(after)

        return carry

    lax.fori_loop(0, applies, apply, 0)


def shards(right_side, fine_blocks, fine_columns, fine_diag, aggregate, coarse_blocks, coarse_diag):
    block_rows, stored, size, _ = fine_blocks.shape
    n_rows = lax.axis_size("rows")
    n_rhs = lax.axis_size("rhs")
    total_blocks = block_rows * n_rows
    groups = n_rhs * coarse_blocks.shape[0]
    per = block_rows // PARTS
    part = per * size
    wide = stored + per
    reach = stored // 2

    local = jnp.arange(block_rows, dtype=jnp.int32)[:, None]
    first = lax.axis_index("rows") * block_rows
    places = jnp.mod(fine_columns - (first + local) + reach, total_blocks) + local % per
    hit = places[:, None, :] == jnp.arange(wide, dtype=jnp.int32)[None, :, None]
    order = jnp.arange(stored, dtype=jnp.int32)[None, None, :]
    found = jnp.max(jnp.where(hit, order, -1), axis=2)
    table = jnp.where(found < 0, stored, found).reshape(block_rows * wide)

    vmem = pl.BlockSpec(memory_space=pltpu.VMEM)
    field = PARTS * part
    geo = (n_rows, n_rhs, block_rows, stored, size)
    return pl.pallas_call(
        functools.partial(kernel, geo),
        out_shape=jax.ShapeDtypeStruct((field, size), F32),
        in_specs=[
            pl.BlockSpec(memory_space=pltpu.SMEM),
            vmem,
            pl.BlockSpec(memory_space=pl.ANY),
            vmem,
            pl.BlockSpec(memory_space=pltpu.SMEM),
            vmem,
            vmem,
        ],
        out_specs=vmem,
        scratch_shapes=[pltpu.VMEM((stored + 1, size, size), BF16) for _ in range(STAGES)]
        + [
            pltpu.VMEM((field, wide * size), BF16),
            pltpu.VMEM((2, PARTS, part, size), BF16),
            pltpu.VMEM((2, PARTS, part, size), BF16),
            pltpu.VMEM((2, PARTS, part, size), BF16),
            pltpu.VMEM((field, size), F32),
            pltpu.VMEM((2, field, size), F32),
            pltpu.VMEM((field, size), F32),
            pltpu.VMEM((field, size), F32),
            pltpu.VMEM((block_rows * groups, size), F32),
            pltpu.VMEM((block_rows * groups, size), F32),
            pltpu.VMEM((block_rows * groups, size), F32),
            pltpu.VMEM((groups, 3, size, size), BF16),
            pltpu.VMEM((groups, 8, size), F32),
            pltpu.VMEM((groups, size, size), F32),
            pltpu.VMEM((groups, size, size), F32),
            pltpu.VMEM((groups, size, size), F32),
            pltpu.VMEM((groups, size, size), F32),
            pltpu.VMEM((CHEB, groups, size, size), BF16),
            pltpu.VMEM((CHEB, groups + 1, size, size), BF16),
            pltpu.VMEM((CHEB, groups + 1, size, size), BF16),
            pltpu.SemaphoreType.DMA((STAGES,)),
            pltpu.SemaphoreType.DMA((2, 2, PARTS)),
            pltpu.SemaphoreType.DMA((2, 2, PARTS)),
            pltpu.SemaphoreType.DMA((2, CHEB, groups)),
            pltpu.SemaphoreType.DMA((2, CHEB, groups)),
            pltpu.SemaphoreType.DMA((2,)),
            pltpu.SemaphoreType.DMA((2,)),
            pltpu.SemaphoreType.DMA((2, n_rhs - 1)),
            pltpu.SemaphoreType.DMA((2, n_rhs - 1)),
        ],
        compiler_params=pltpu.CompilerParams(
            collective_id=0, has_side_effects=True, vmem_limit_bytes=56 * 1024 * 1024
        ),
    )(
        table,
        right_side,
        fine_blocks,
        fine_diag.reshape(block_rows, size),
        aggregate,
        coarse_blocks[0],
        coarse_diag.reshape(1, size),
    )


def solution(mesh):
    in_specs = (
        P("rows", "rhs"),
        P("rows", None, None, None),
        P("rows", None),
        P("rows"),
        P("rows"),
        P(("rhs", "rows"), None, None, None),
        P(("rhs", "rows")),
    )
    out_specs = P("rows", "rhs")
    return jax.shard_map(shards, mesh=mesh, in_specs=in_specs, out_specs=out_specs, check_vma=False)
```
